32 devices in a mesh: groups: 2 (over x), slab: 16 (over z, y, core).
Axes of the slice: x: 2, y: 2, z: 4, core: 2. Of those that a mesh axis runs over, the one named last changes fastest.
Arguments:
- point_pos: float32 [3, 131072], P(None, ('groups', 'slab')), parts along dimension 1, may hold values from 0 to 1
- point_input: float32 [8, 131072], P(None, ('groups', 'slab')), parts along dimension 1, may hold values from -6 to 6
- req_owner: int32 [16384, 1], P(('groups', 'slab')), parts along dimension 0, may hold values from 0 to 15; in each aligned block of 512 rows (0 to 511, 512 to 1023, ...) at most 128 rows name the same one
- req_local: int32 [16384], P(('groups', 'slab')), parts along dimension 0, may hold values from 0 to 4095
- pair_cell: int32 [128], P(('groups', 'slab')), parts along dimension 0, may hold values from 0 to 1
- pair_mask: int32 [128, 64, 128], P(('groups', 'slab')), parts along dimension 0, may hold values 0 or 1
- w_first: float32 [7, 256], replicated, may hold values from -2.5 to 2.5
- w_second: bfloat16 [256, 64], replicated, may hold values from -1.5 to 1.5
- w_lift: float32 [8, 64], replicated, may hold values from -2 to 2
- cotangent: float32 [64, 4096], P(None, ('groups', 'slab')), parts along dimension 1, may hold values from -6 to 6
Outputs:
- latent: bfloat16 [64, 4096], P(None, ('groups', 'slab')), parts along dimension 1
- grad_first: float32 [14, 256], P('groups'), parts along dimension 0
- grad_second: float32 [512, 64], P('groups'), parts along dimension 0
- grad_lift: float32 [16, 64], P('groups'), parts along dimension 0
The draws below stay inside these ranges and needn't reach their ends.
There are 2 independent parts, one for each index of `groups`. The reference program is written for one: setup_inputs(seed, part) draws one part's arguments, and reference() takes and returns one part's arrays. A program takes and returns all parts, laid end to end along the dimension named above; an argument that names none is the same for every part. Nothing has to cross between parts.
Inputs may be any that keep to these rules, and one draw needn't show every extreme that they name: `req_owner`: within the 512 rows of one slab (aligned blocks), no partition is named more than 128 times.
All inputs are finite; a program needn't handle non-finite values. No bound on the sum of `pair_mask` on one device may be relied on, other than what follows from the above.
Results may differ from the reference program's by a relative error of at most 0.0034.
Values sent between devices are 32-bit elements; how exact they have to be, the bound alone decides.
A program may use at most 64 MiB of HBM per device.

```python
import math
import jax
import jax.numpy as jnp
import numpy as np
from jax import lax

CHANNELS = 64
HIDDEN_SIZE = 256
INPUTS = 8
BLOCK_PTS = 128
BLOCK_CELLS = 64
GRID_ROW = 16
PTS_DEV = 4096
PAIRS_DEV = 4
BLOCKS_DEV = 2
REQ_DEV = 512
CAPACITY = 128
CELLS_DEV = 128
POINTS = 65536
PAIRS = 64
REQUESTS = 8192
CELLS = 2048
N_SLAB = 16


def with_ends(entries, rng, smallest, top_value):
    place = [jax.random.randint(jax.random.fold_in(rng, axis), (), 0, length) for axis, length in enumerate(entries.shape)]
    widest = entries.shape.index(max(entries.shape))
    next_to = place[:widest] + [(place[widest] + 1) % entries.shape[widest]] + place[widest + 1:]
    return entries.at[tuple(place)].set(smallest).at[tuple(next_to)].set(top_value)


def shard_levels(key, extent, shards, least, high):
    factor_of, own = 1.0, jax.random.fold_in(key, 6)
    for axis_at, shards_of in shards:
        draws = jnp.exp(jax.random.uniform(jax.random.fold_in(own, axis_at), (shards_of,), jnp.float32, least / len(shards), high / len(shards)))
        factor_of = factor_of * jnp.repeat(draws, extent[axis_at] // shards_of).reshape([-1 if axis == axis_at else 1 for axis in range(len(extent))])
    return factor_of


def shared_out(stream_key, own, number, rows, number_of, top, bound, lean):
    ranking = jax.random.permutation(stream_key, number_of)
    packed, usual = shares(number_of, rows * top, bound, lean, True), shares(number_of, rows * top, bound, lean, False)
    places = jnp.arange(number_of)

    def named(sizes, offset_by):
        used = int((sizes > 0).sum())
        fixed = max(1, used // 4)
        passed = fixed + (places - fixed + offset_by * (used - fixed)) % max(1, number_of - fixed)
        return jnp.zeros((number_of,), jnp.int32).at[ranking[jnp.where(places < fixed, places, passed)]].set(jnp.asarray(sizes, jnp.int32))

    sizes = jnp.where(number % 4 == 0, named(packed, number // 4), named(usual, number - number // 4 - 1))
    mixed = jax.random.permutation(jax.random.fold_in(own, 3), number_of)
    source_of, sink = mixed[0:number_of // 2 * 2:2], mixed[1:number_of // 2 * 2:2]
    slack = jnp.minimum(sizes[source_of] - 1, bound - sizes[sink]) // 2
    slack = jnp.where((source_of == ranking[0]) | (sink == ranking[0]) | (sizes[sink] == 0), 0, jnp.maximum(slack, 0))
    passed = jax.random.randint(jax.random.fold_in(own, 4), (number_of // 2,), 0, 1 << 20) % (slack + 1)
    sizes = sizes.at[source_of].add(-passed).at[sink].add(passed)
    items = jnp.searchsorted(jnp.cumsum(sizes), jnp.arange(rows * top), side="right").astype(jnp.int32)
    listing = items.reshape(top, rows).T
    listing = listing[jax.random.permutation(jax.random.fold_in(own, 1), rows)]
    offset_by = jax.random.randint(jax.random.fold_in(own, 2), (rows, 1), 0, top)
    return jnp.take_along_axis(listing, (jnp.arange(top)[None, :] + offset_by) % top, axis=1)


def shares(count, total, most, slope, full):
    weights = [(1 << 20) // math.isqrt(standing ** slope) + 1 for standing in range(1, count + 1)]
    largest = most if full else min(most, max(-(-total // count), total * weights[0] // sum(weights)))
    least = 1 if total - largest >= count - 1 else 0
    holding, rest = [largest] + [least] * (count - 1), total - largest - least * (count - 1)
    while rest > 0:
        free = [i for i in range(1, count) if holding[i] < largest] or [i for i in range(1, count) if holding[i] < most]
        pool, budget = sum([weights[i] for i in free]), rest
        for i in free:
            addition = min(most - holding[i], max(1, budget * weights[i] // pool), rest)
            holding[i] = holding[i] + addition
            rest = rest - addition
    return np.array(holding)


def scatter_about(key, dims, scale, limit, cuts=(), kind=jnp.bfloat16):
    values = scale * jax.random.normal(key, dims, jnp.float32)
    if cuts:
        values = values * shard_levels(key, dims, cuts, -0.22, 0.18)
    return jnp.clip(values, -limit, limit).astype(kind)


def setup_inputs(seed: int = 0, part: int = 0) -> dict:
    key_list = jax.random.split(jax.random.key(seed), 11)
    part_keys = jax.random.split(jax.random.fold_in(key_list[10], part), 11)
    point_pos = jnp.clip(1.0 * jax.random.uniform(part_keys[0], (3, POINTS), jnp.float32) ** shard_levels(part_keys[0], (3, POINTS), ((1, 16),), -0.2, 0.2), 0.0, 1.0)
    point_input = scatter_about(part_keys[1], (INPUTS, POINTS), 1.0, 6.0, ((1, 16),), jnp.float32)
    req_owner_keys = jax.random.split(jax.random.fold_in(part_keys[2], 1), REQUESTS // REQ_DEV)
    req_owner_turns = jax.random.permutation(jax.random.fold_in(part_keys[2], 3), REQUESTS // REQ_DEV)
    req_owner = jax.vmap(lambda own, number: shared_out(jax.random.fold_in(part_keys[2], 2), own, number, REQ_DEV, N_SLAB, 1, CAPACITY, 2))(req_owner_keys, req_owner_turns).reshape((REQUESTS, 1))
    req_local = with_ends(jax.random.randint(part_keys[3], (REQUESTS,), 0, PTS_DEV), jax.random.fold_in(part_keys[3], 1), 0, PTS_DEV - 1).astype(jnp.int32)
    pair_cell = with_ends(jax.random.randint(part_keys[4], (PAIRS,), 0, BLOCKS_DEV), jax.random.fold_in(part_keys[4], 1), 0, BLOCKS_DEV - 1).astype(jnp.int32)
    pair_mask = with_ends((jax.random.randint(part_keys[5], (PAIRS, BLOCK_CELLS, BLOCK_PTS), 0, 2) < 1).astype(jnp.int32), jax.random.fold_in(part_keys[5], 1), 0, 1)
    w_first = scatter_about(key_list[6], (7, HIDDEN_SIZE), 6 ** -0.5, 2.5, (), jnp.float32)
    w_second = scatter_about(key_list[7], (HIDDEN_SIZE, CHANNELS), 0.25, 1.5)
    w_lift = scatter_about(key_list[8], (INPUTS, CHANNELS), INPUTS ** -0.5, 2.0, (), jnp.float32)
    cotangent = scatter_about(part_keys[9], (CHANNELS, CELLS), 1.0, 6.0, ((1, 16),), jnp.float32)
    return dict(point_pos=point_pos, point_input=point_input, req_owner=req_owner, req_local=req_local, pair_cell=pair_cell, pair_mask=pair_mask, w_first=w_first, w_second=w_second, w_lift=w_lift, cotangent=cotangent)


PREC = lax.Precision.HIGHEST

def silu_slope(values):
    sig = jax.nn.sigmoid(values)
    return sig * (1.0 + values * (1.0 - sig))

def cell_coords(local, slab_id, cells_dev, slab_count, grid_row):
    column = (local % grid_row).astype(jnp.float32)
    row_idx = (local // grid_row).astype(jnp.float32)
    first = (column + 0.5) / grid_row
    second = (row_idx + 0.5) * grid_row / cells_dev
    third = (slab_id.astype(jnp.float32) + 0.5) / slab_count + 0.0 * first
    return jnp.stack([first, second, third])

def pair_terms(points_y, feats, cells_x, mask, gcell, w_first, w_second):
    point_part = jnp.dot(points_y.T, w_first[0:3], precision=PREC, preferred_element_type=jnp.float32)
    cell_part = jnp.dot(cells_x.T, w_first[3:6], precision=PREC, preferred_element_type=jnp.float32) + w_first[6]
    n_cells = cell_part.shape[0]
    n_points = point_part.shape[0]
    width = point_part.shape[1]
    preact = (cell_part[:, None, :] + point_part[None, :, :]).reshape(n_cells * n_points, width)
    activ, slope_fn = jax.vjp(jax.nn.gelu, preact)
    hidden = activ.astype(jnp.bfloat16)
    kernel = lax.dot_general(w_second, hidden, (((0,), (1,)), ((), ())), preferred_element_type=jnp.float32)
    kernel = kernel.reshape(-1, n_cells, n_points)
    weighted = mask[None, :, :] * feats[:, None, :]
    contrib = lax.optimization_barrier(jnp.sum(kernel * weighted, axis=2))
    dkernel = (weighted * gcell[:, :, None]).astype(jnp.bfloat16).reshape(-1, n_cells * n_points)
    dfeat = lax.optimization_barrier(jnp.sum(kernel * mask[None, :, :] * gcell[:, :, None], axis=1))
    dsecond = lax.dot_general(hidden, dkernel, (((0,), (1,)), ((), ())), preferred_element_type=jnp.float32)
    dhidden = lax.dot_general(dkernel, w_second, (((0,), (1,)), ((), ())), preferred_element_type=jnp.float32)
    dpre = slope_fn(dhidden)[0].reshape(n_cells, n_points, width)
    per_point = lax.optimization_barrier(jnp.sum(dpre, axis=0))
    per_cell = lax.optimization_barrier(jnp.sum(dpre, axis=1))
    dfirst = jnp.concatenate([jnp.dot(points_y, per_point, precision=PREC, preferred_element_type=jnp.float32), jnp.dot(cells_x, per_cell, precision=PREC, preferred_element_type=jnp.float32), lax.optimization_barrier(jnp.sum(per_cell, axis=0, keepdims=True))], axis=0)
    return (contrib, dfeat, dfirst, dsecond)

def reference(point_pos, point_input, req_owner, req_local, pair_cell, pair_mask, w_first, w_second, w_lift, cotangent):
    point_ids = req_owner[:, 0] * PTS_DEV + req_local
    req_pos = point_pos[:, point_ids]
    req_input = point_input[:, point_ids]
    req_z = jnp.dot(w_lift.T, req_input, precision=PREC, preferred_element_type=jnp.float32)
    req_feat = jax.nn.silu(req_z)
    mask_float = pair_mask.astype(jnp.float32)
    pair_total = pair_mask.shape[0]
    owner_slab = jnp.arange(pair_total, dtype=jnp.int32) // PAIRS_DEV
    block_ids = owner_slab * BLOCKS_DEV + pair_cell
    block_total = BLOCKS_DEV * N_SLAB
    counts = jax.ops.segment_sum(lax.optimization_barrier(jnp.sum(mask_float, axis=2)), block_ids, num_segments=block_total)
    divisor = jnp.maximum(counts, 1.0)
    gcells = cotangent.reshape(CHANNELS, block_total, BLOCK_CELLS) / divisor[None, :, :]
    cell_index = jnp.arange(CELLS, dtype=jnp.int32)
    cells_all = cell_coords(cell_index % CELLS_DEV, cell_index // CELLS_DEV, CELLS_DEV, N_SLAB, GRID_ROW)
    cells_all = cells_all.reshape(3, block_total, BLOCK_CELLS)
    pair_pos = req_pos.reshape(3, pair_total, BLOCK_PTS).transpose(1, 0, 2)
    pair_feat = req_feat.reshape(CHANNELS, pair_total, BLOCK_PTS).transpose(1, 0, 2)
    pair_cells = cells_all[:, block_ids].transpose(1, 0, 2)
    pair_grads = gcells[:, block_ids].transpose(1, 0, 2)

    def per_pair(pieces):
        return pair_terms(pieces[0], pieces[1], pieces[2], pieces[3], pieces[4], w_first, w_second)
    contrib, dfeat, dfirst, dsecond = lax.map(per_pair, (pair_pos, pair_feat, pair_cells, mask_float, pair_grads))
    summed = jax.ops.segment_sum(contrib, block_ids, num_segments=block_total)
    latent = (summed / divisor[:, None, :]).transpose(1, 0, 2).reshape(CHANNELS, CELLS).astype(jnp.bfloat16)
    req_grad = dfeat.transpose(1, 0, 2).reshape(CHANNELS, pair_total * BLOCK_PTS)
    grad_lift = jnp.dot(req_input, (req_grad * silu_slope(req_z)).T, precision=PREC, preferred_element_type=jnp.float32)
    return (latent, lax.optimization_barrier(jnp.sum(dfirst, axis=0)), lax.optimization_barrier(jnp.sum(dsecond, axis=0)), grad_lift)
```

```python
import functools

import jax
import jax.numpy as jnp
from jax import lax
from jax.experimental import pallas as pl
from jax.experimental.pallas import tpu as pltpu
from jax.sharding import PartitionSpec as P

BLOCK_PTS = 128
BLOCK_CELLS = 64
GRID_ROW = 16
GROUP = 8
CHUNK = 64
GELU_A = 0.7978845608028654
GELU_B = 0.044715 * GELU_A

PREC = lax.Precision.HIGHEST
F32 = jnp.float32
BF16 = jnp.bfloat16


def nn(a, b):
    return lax.dot_general(a, b, (((1,), (0,)), ((), ())), preferred_element_type=F32)


def nt(a, b, precision=None):
    return lax.dot_general(
        a, b, (((1,), (1,)), ((), ())), precision=precision, preferred_element_type=F32
    )


def tn_exact(a, b):
    return lax.dot_general(
        a, b, (((0,), (0,)), ((), ())), precision=PREC, preferred_element_type=F32
    )


def halves(value):
    high = value.astype(BF16)
    return high, (value - high.astype(F32)).astype(BF16)


def iota(shape, axis):
    return lax.broadcasted_iota(jnp.int32, shape, axis)


def body(
    peers,
    pos_ref,
    input_ref,
    owner_ref,
    local_ref,
    pair_ref,
    mask_ref,
    first_ref,
    second_ref,
    lift_ref,
    cot_ref,
    latent_ref,
    gfirst_ref,
    gsecond_ref,
    glift_ref,
    place_ref,
    want_out,
    want_in,
    table_ref,
    reply_out,
    reply_in,
    cellpart_ref,
    gcell_ref,
    cellrow_ref,
    pointpart_ref,
    feat_ref,
    yrow_ref,
    dk_ref,
    dh_ref,
    hid_ref,
    dpre_ref,
    lat_ref,
    dfeat_ref,
    dsec_ref,
    dfir_ref,
    flat_ref,
    part_out,
    part_in,
    total_out,
    total_in,
    want_send,
    want_recv,
    reply_send,
    reply_recv,
    part_send,
    part_recv,
    total_send,
    total_recv,
):
    me = lax.axis_index("slab")
    req_count = local_ref.shape[1]
    capacity = want_in.shape[2]
    pairs = mask_ref.shape[0]
    cells = cot_ref.shape[1]
    blocks = cells // BLOCK_CELLS
    groups = BLOCK_CELLS // GROUP
    channels = cot_ref.shape[0]
    width = first_ref.shape[1]
    share = part_in.shape[1]

    barrier = pltpu.get_barrier_semaphore()

    def greet(step, carry):
        peer = lax.rem(me + step, peers)
        pl.semaphore_signal(barrier, inc=1, device_id={"slab": peer})
        return carry

    lax.fori_loop(1, peers, greet, 0)

    def exchange(source, target, send, recv, step):
        peer = lax.rem(me + step, peers)
        return pltpu.make_async_remote_copy(
            src_ref=source.at[peer],
            dst_ref=target.at[me],
            send_sem=send.at[peer],
            recv_sem=recv.at[me],
            device_id={"slab": peer},
        )

    def arrival(target, send, recv, step):
        peer = lax.rem(me + step, peers)
        return peer, pltpu.make_async_remote_copy(
            src_ref=target.at[peer],
            dst_ref=target.at[peer],
            send_sem=send.at[peer],
            recv_sem=recv.at[peer],
            device_id={"slab": peer},
        )

    owner = owner_ref[...]
    local = local_ref[...]
    named = jnp.where(owner == iota((peers, req_count), 0), 1.0, 0.0)
    earlier = jnp.where(
        iota((req_count, req_count), 0) < iota((req_count, req_count), 1), 1.0, 0.0
    ).astype(BF16)
    rank = jnp.sum(named * nn(named.astype(BF16), earlier), axis=0, keepdims=True)
    slot = owner * capacity + rank.astype(jnp.int32)
    line = iota((16, req_count), 0)
    digits = jnp.where(
        line == 0, local >> 7, jnp.where(line == 1, local & 127, 0)
    ).astype(F32).astype(BF16)
    for p in range(peers):
        place = jnp.where(
            slot == p * capacity + iota((capacity, req_count), 0), 1.0, 0.0
        ).astype(BF16)
        place_ref[p] = place
        found = nt(digits, place)
        want_out[p] = (found[0:1] * 128.0 + found[1:2]).astype(jnp.int32)

    pl.semaphore_wait(barrier, peers - 1)

    def ask(step, carry):
        exchange(want_out, want_in, want_send, want_recv, step).start()
        return carry

    lax.fori_loop(1, peers, ask, 0)
    want_in[me] = want_out[me]

    highs = input_ref.shape[1] // 128
    for h in range(highs):
        lanes = slice(h * 128, (h + 1) * 128)
        upper, lower = halves(input_ref[:, lanes])
        table_ref[h * 16 : h * 16 + 8, 0:128] = upper
        table_ref[h * 16 : h * 16 + 8, 128:256] = lower
        coords = jnp.concatenate([pos_ref[:, lanes], jnp.zeros((5, 128), F32)], axis=0)
        upper, lower = halves(coords)
        table_ref[h * 16 + 8 : h * 16 + 16, 0:128] = upper
        table_ref[h * 16 + 8 : h * 16 + 16, 128:256] = lower

    def provide(peer):
        wanted = want_in[peer]
        one = jnp.where((wanted & 127) == iota((128, capacity), 0), 1.0, 0.0).astype(BF16)
        rows = nn(table_ref[...], jnp.concatenate([one, one], axis=0))
        rows = rows.reshape(highs, 16, capacity)
        chosen = (wanted >> 7) == iota((highs, 1, capacity), 0)
        rows = jnp.sum(jnp.where(chosen, rows, 0.0), axis=0)
        reply_out[peer] = rows[0 : reply_out.shape[1]]

    provide(me)

    def answer(step, carry):
        peer, got = arrival(want_in, want_send, want_recv, peers - step)
        got.wait_recv()
        provide(peer)
        exchange(reply_out, reply_in, reply_send, reply_recv, peers - step).start()
        return carry

    lax.fori_loop(1, peers, answer, 0)
    reply_in[me] = reply_out[me]

    counts = []
    ones = jnp.ones((16, BLOCK_PTS), BF16)
    per_pair = [nt(ones, mask_ref[j].astype(F32).astype(BF16))[0:1] for j in range(pairs)]
    for b in range(blocks):
        count = jnp.zeros((1, BLOCK_CELLS), F32)
        for j in range(pairs):
            count = count + jnp.where(pair_ref[j] == b, per_pair[j], 0.0)
        counts.append(count)
    divisor = jnp.maximum(jnp.concatenate(counts, axis=1), 1.0)
    gcells = cot_ref[...] / divisor
    index = iota((16, cells), 1)
    column = (lax.rem(index, GRID_ROW).astype(F32) + 0.5) / GRID_ROW
    row = (lax.div(index, GRID_ROW).astype(F32) + 0.5) * GRID_ROW / cells
    third = (me.astype(F32) + 0.5) / peers
    line = iota((16, cells), 0)
    coords = jnp.where(line == 0, column, jnp.where(line == 1, row, third))
    shifted = jnp.where(
        line == 3,
        column,
        jnp.where(
            line == 4, row, jnp.where(line == 5, third, jnp.where(line == 6, 1.0, 0.0))
        ),
    )
    first = first_ref[...]
    cell_weights = jnp.concatenate([first[3:7], jnp.zeros((4, width), F32)], axis=0)
    cell_values = jnp.where(line == 3, 1.0, jnp.where(line < 3, coords, 0.0))[0:8]
    cellpart = tn_exact(cell_weights, cell_values)
    for k in range(blocks * groups):
        turn = (cells - k * GROUP) % cells
        for value, into in ((cellpart, cellpart_ref), (gcells, gcell_ref), (shifted, cellrow_ref)):
            into[k] = pltpu.roll(value, turn, 1) if turn else value
    half_second = (second_ref[...].astype(F32) * 0.5)
    half_turned = half_second.T.astype(BF16)
    half_second = half_second.astype(BF16)
    lat_ref[...] = jnp.zeros_like(lat_ref)
    dsec_ref[...] = jnp.zeros_like(dsec_ref)
    dfir_ref[...] = jnp.zeros_like(dfir_ref)
    dfeat_ref[...] = jnp.zeros_like(dfeat_ref)

    def settle(step, carry):
        peer, got = arrival(reply_in, reply_send, reply_recv, step)
        got.wait()
        _, sent = arrival(want_in, want_send, want_recv, step)
        sent.wait_send()
        return carry

    lax.fori_loop(1, peers, settle, 0)
    read = jnp.zeros((reply_in.shape[1], req_count), F32)
    for p in range(peers):
        upper, lower = halves(reply_in[p])
        read = read + (nn(upper, place_ref[p]) + nn(lower, place_ref[p]))
    inputs = read[0:8]
    points = jnp.concatenate([read[8:11], jnp.zeros((5, req_count), F32)], axis=0)
    req_z = tn_exact(lift_ref[...], inputs)
    gate = jax.nn.sigmoid(req_z)
    feats = req_z * gate
    slope = gate * (1.0 + req_z * (1.0 - gate))
    point_weights = jnp.concatenate([first[0:3], jnp.zeros((5, width), F32)], axis=0)
    pointpart = tn_exact(point_weights, points)
    upper = points.astype(BF16).astype(F32)
    both = jnp.concatenate([upper, points - upper], axis=0)
    for j in range(pairs):
        lanes = slice(j * BLOCK_PTS, (j + 1) * BLOCK_PTS)
        feat_ref[j] = feats[:, lanes]
        pointpart_ref[j] = pointpart[:, lanes]
        yrow_ref[j] = both[:, lanes]

    def work(step, carry):
        j = step // groups
        i = step % groups
        cell_block = pair_ref[j]
        at = cell_block * groups + i
        mask = mask_ref[j, pl.ds(pl.multiple_of(i * GROUP, GROUP), GROUP), :].astype(F32)
        feat = feat_ref[j]
        grads = gcell_ref[at]
        for s in range(GROUP):
            lanes = slice(s * BLOCK_PTS, (s + 1) * BLOCK_PTS)
            dk_ref[:, lanes] = ((feat * mask[s : s + 1]) * grads[:, s : s + 1]).astype(BF16)
        for s in range(0, GROUP, 2):
            lanes = slice(s * BLOCK_PTS, (s + 2) * BLOCK_PTS)
            dh_ref[:, lanes] = nn(half_second, dk_ref[:, lanes])
        for s in range(GROUP):
            lanes = slice(s * BLOCK_PTS, (s + 1) * BLOCK_PTS)
            for h in range(0, width, CHUNK):
                rows = slice(h, h + CHUNK)
                x = pointpart_ref[j, rows, :] + cellpart_ref[at, rows, s : s + 1]
                square = x * x
                t = jnp.tanh(x * (GELU_A + GELU_B * square))
                u = 1.0 + t
                hid = x * u
                hid_ref[rows, lanes] = hid.astype(BF16)
                bend = hid * (1.0 - t) * (GELU_A + (3.0 * GELU_B) * square)
                dpre_ref[rows, lanes] = ((u + bend) * dh_ref[rows, lanes]).astype(BF16)
        lat = jnp.zeros((channels, cells), F32)
        dfeat = jnp.zeros((channels, BLOCK_PTS), F32)
        lane = iota((channels, cells), 1)
        sides = []
        for s in range(0, GROUP, 2):
            pair_lanes = slice(s * BLOCK_PTS, (s + 2) * BLOCK_PTS)
            kernels = nn(half_turned, hid_ref[:, pair_lanes])
            for d in range(2):
                c = s + d
                masked = kernels[:, d * BLOCK_PTS : (d + 1) * BLOCK_PTS] * mask[c : c + 1]
                total = jnp.sum(masked * feat, axis=1, keepdims=True)
                lat = lat + jnp.where(
                    lane == cell_block * BLOCK_CELLS + i * GROUP + c, total, 0.0
                )
                dfeat = dfeat + masked * grads[:, c : c + 1]
                sides.append((yrow_ref[j] + cellrow_ref[at][:, c : c + 1]).astype(BF16))
        lat_ref[...] += lat
        dfeat_ref[j] += dfeat
        dsec_ref[...] += nt(dk_ref[...], hid_ref[...])
        dfir_ref[...] += nt(jnp.concatenate(sides, axis=1), dpre_ref[...])
        return carry

    lax.fori_loop(0, pairs * groups, work, 0)

    latent_ref[...] = (lat_ref[...] / divisor).astype(BF16)
    dfeat = jnp.concatenate([dfeat_ref[j] for j in range(pairs)], axis=1)
    lift = nt(inputs, dfeat * slope, PREC)
    half = width // 2
    flat_ref[...] = jnp.zeros_like(flat_ref)
    dsec = dsec_ref[...] * 0.5
    dfir = dfir_ref[0:8] + dfir_ref[8:16]
    flat_ref[0:channels] = dsec[:, :half]
    flat_ref[channels : 2 * channels] = dsec[:, half:]
    flat_ref[2 * channels : 2 * channels + 8] = dfir[:, :half]
    flat_ref[2 * channels + 8 : 2 * channels + 16] = dfir[:, half:]
    flat_ref[2 * channels + 16 : 2 * channels + 24, 0:channels] = lift
    for p in range(peers):
        part_out[p] = flat_ref[p * share : (p + 1) * share]

    def scatter(step, carry):
        exchange(part_out, part_in, part_send, part_recv, step).start()
        return carry

    lax.fori_loop(1, peers, scatter, 0)
    part_in[me] = part_out[me]

    def take(step, carry):
        _, got = arrival(part_in, part_send, part_recv, step)
        got.wait()
        return carry

    lax.fori_loop(1, peers, take, 0)
    total_out[...] = jnp.sum(part_in[...], axis=0)

    def spread(step):
        peer = lax.rem(me + step, peers)
        return pltpu.make_async_remote_copy(
            src_ref=total_out,
            dst_ref=total_in.at[me],
            send_sem=total_send.at[peer],
            recv_sem=total_recv.at[me],
            device_id={"slab": peer},
        )

    def give(step, carry):
        spread(step).start()
        return carry

    lax.fori_loop(1, peers, give, 0)
    total_in[me] = total_out[...]

    def collect(step, carry):
        _, got = arrival(total_in, total_send, total_recv, step)
        got.wait()
        return carry

    lax.fori_loop(1, peers, collect, 0)
    for p in range(peers):
        flat_ref[p * share : (p + 1) * share] = total_in[p]
    gsecond_ref[0:half] = flat_ref[0:channels].T
    gsecond_ref[half:width] = flat_ref[channels : 2 * channels].T
    gfirst_ref[:, 0:half] = flat_ref[2 * channels : 2 * channels + 7]
    gfirst_ref[:, half:width] = flat_ref[2 * channels + 8 : 2 * channels + 15]
    glift_ref[...] = flat_ref[2 * channels + 16 : 2 * channels + 24, 0:channels]


def per_device(
    point_pos,
    point_input,
    req_owner,
    req_local,
    pair_cell,
    pair_mask,
    w_first,
    w_second,
    w_lift,
    cotangent,
):
    peers = lax.axis_size("slab")
    req_count = req_local.shape[0]
    capacity = 4 * req_count // peers
    channels, cells = cotangent.shape
    width = w_first.shape[1]
    pairs = pair_mask.shape[0]
    points = point_input.shape[1]
    rows = point_input.shape[0] + point_pos.shape[0]
    kinds = cells // GROUP
    share = -(-(2 * channels + 24) // peers)
    span = GROUP * BLOCK_PTS
    vmem = pl.BlockSpec(memory_space=pltpu.VMEM)
    sems = [pltpu.SemaphoreType.DMA((peers,))] * 8
    return pl.pallas_call(
        functools.partial(body, peers),
        out_shape=(
            jax.ShapeDtypeStruct((channels, cells), BF16),
            jax.ShapeDtypeStruct(w_first.shape, F32),
            jax.ShapeDtypeStruct(w_second.shape, F32),
            jax.ShapeDtypeStruct(w_lift.shape, F32),
        ),
        in_specs=[vmem] * 4 + [pl.BlockSpec(memory_space=pltpu.SMEM)] + [vmem] * 5,
        out_specs=[vmem] * 4,
        scratch_shapes=[
            pltpu.VMEM((peers, capacity, req_count), BF16),
            pltpu.VMEM((peers, 1, capacity), jnp.int32),
            pltpu.VMEM((peers, 1, capacity), jnp.int32),
            pltpu.VMEM((points // 128 * 16, 256), BF16),
            pltpu.VMEM((peers, rows, capacity), F32),
            pltpu.VMEM((peers, rows, capacity), F32),
            pltpu.VMEM((kinds, width, cells), F32),
            pltpu.VMEM((kinds, channels, cells), F32),
            pltpu.VMEM((kinds, 16, cells), F32),
            pltpu.VMEM((pairs, width, BLOCK_PTS), F32),
            pltpu.VMEM((pairs, channels, BLOCK_PTS), F32),
            pltpu.VMEM((pairs, 16, BLOCK_PTS), F32),
            pltpu.VMEM((channels, span), BF16),
            pltpu.VMEM((width, span), F32),
            pltpu.VMEM((width, span), BF16),
            pltpu.VMEM((width, span), BF16),
            pltpu.VMEM((channels, cells), F32),
            pltpu.VMEM((pairs, channels, BLOCK_PTS), F32),
            pltpu.VMEM((channels, width), F32),
            pltpu.VMEM((16, width), F32),
            pltpu.VMEM((peers * share, 128), F32),
            pltpu.VMEM((peers, share, 128), F32),
            pltpu.VMEM((peers, share, 128), F32),
            pltpu.VMEM((share, 128), F32),
            pltpu.VMEM((peers, share, 128), F32),
        ]
        + sems,
        compiler_params=pltpu.CompilerParams(
            collective_id=0, has_side_effects=True, vmem_limit_bytes=40 * 1024 * 1024
        ),
    )(
        point_pos,
        point_input,
        req_owner.reshape(1, req_count),
        req_local.reshape(1, req_count),
        pair_cell,
        pair_mask,
        w_first,
        w_second,
        w_lift,
        cotangent,
    )


def solution(mesh):
    split = ("groups", "slab")
    in_specs = (
        P(None, split),
        P(None, split),
        P(split, None),
        P(split),
        P(split),
        P(split, None, None),
        P(),
        P(),
        P(),
        P(None, split),
    )
    out_specs = (P(None, split), P("groups", None), P("groups", None), P("groups", None))
    return jax.shard_map(
        per_device, mesh=mesh, in_specs=in_specs, out_specs=out_specs, check_vma=False
    )
```

```python
import functools

import ml_dtypes
import numpy as np
import jax
import jax.numpy as jnp
from jax import lax
from jax.experimental import pallas as pl
from jax.experimental.pallas import tpu as pltpu
from jax.sharding import PartitionSpec as P

BLOCK_PTS = 128
BLOCK_CELLS = 64
GRID_ROW = 16
GROUP = 8
CHUNK = 64
GELU_A = 0.7978845608028654
GELU_B = 0.044715 * GELU_A

ONE = np.array(1.0, ml_dtypes.bfloat16)
A16 = np.array(GELU_A, ml_dtypes.bfloat16)
B16 = np.array(GELU_B, ml_dtypes.bfloat16)
C16 = np.array(3.0*GELU_B, ml_dtypes.bfloat16)
PREC = lax.Precision.HIGHEST
F32 = jnp.float32
BF16 = jnp.bfloat16


def nn(a, b):
    return lax.dot_general(a, b, (((1,), (0,)), ((), ())), preferred_element_type=F32)


def nt(a, b, precision=None):
    return lax.dot_general(
        a, b, (((1,), (1,)), ((), ())), precision=precision, preferred_element_type=F32
    )


def tn_exact(a, b):
    return lax.dot_general(
        a, b, (((0,), (0,)), ((), ())), precision=PREC, preferred_element_type=F32
    )


def halves(value):
    high = value.astype(BF16)
    return high, (value - high.astype(F32)).astype(BF16)


def iota(shape, axis):
    return lax.broadcasted_iota(jnp.int32, shape, axis)


def body(
    peers,
    pos_ref,
    input_ref,
    owner_ref,
    local_ref,
    pair_ref,
    mask_ref,
    first_ref,
    second_ref,
    lift_ref,
    cot_ref,
    latent_ref,
    gfirst_ref,
    gsecond_ref,
    glift_ref,
    place_ref,
    want_out,
    want_in,
    table_ref,
    reply_out,
    reply_in,
    cellpart_ref,
    gcell_ref,
    cellrow_ref,
    pointpart_ref,
    feat_ref,
    yrow_ref,
    dk_ref,
    dh_ref,
    hid_ref,
    dpre_ref,
    side_ref,
    wpre_ref,
    lat_ref,
    dfeat_ref,
    dsec_ref,
    dfir_ref,
    flat_ref,
    part_out,
    part_in,
    total_out,
    total_in,
    want_send,
    want_recv,
    reply_send,
    reply_recv,
    part_send,
    part_recv,
    total_send,
    total_recv,
):
    me = lax.axis_index("slab")
    req_count = local_ref.shape[1]
    capacity = want_in.shape[2]
    pairs = mask_ref.shape[0]
    cells = cot_ref.shape[1]
    blocks = cells // BLOCK_CELLS
    groups = BLOCK_CELLS // GROUP
    channels = cot_ref.shape[0]
    width = first_ref.shape[1]
    share = part_in.shape[1]

    barrier = pltpu.get_barrier_semaphore()

    def loop(act):
        lax.fori_loop(1, peers, act, 0, unroll=1)

    def greet(step, carry):
        peer = lax.rem(me + step, peers)
        pl.semaphore_signal(barrier, inc=1, device_id={"slab": peer})
        return carry

    loop(greet)

    def exchange(source, target, send, recv, step):
        peer = lax.rem(me + step, peers)
        return pltpu.make_async_remote_copy(
            src_ref=source.at[peer],
            dst_ref=target.at[me],
            send_sem=send,
            recv_sem=recv.at[me] if recv is want_recv else recv,
            device_id={"slab": peer},
        )

    def drain(like, sem):
        part = like.at[pl.ds(0, peers - 1)]
        pltpu.make_async_copy(part, part, sem).wait()

    def arrival(target, send, recv, step):
        peer = lax.rem(me + step, peers)
        return peer, pltpu.make_async_remote_copy(
            src_ref=target.at[peer],
            dst_ref=target.at[peer],
            send_sem=send,
            recv_sem=recv.at[peer],
            device_id={"slab": peer},
        )

    owner = owner_ref[...]
    local = local_ref[...]
    named = jnp.where(owner == iota((peers, req_count), 0), 1.0, 0.0)
    earlier = jnp.where(
        iota((req_count, req_count), 0) < iota((req_count, req_count), 1), 1.0, 0.0
    ).astype(BF16)
    rank = jnp.sum(named * nn(named.astype(BF16), earlier), axis=0, keepdims=True)
    slot = owner * capacity + rank.astype(jnp.int32)
    line = iota((16, req_count), 0)
    digits = jnp.where(
        line == 0, local >> 7, jnp.where(line == 1, local & 127, 0)
    ).astype(F32).astype(BF16)
    for p in range(peers):
        place = jnp.where(
            slot == p * capacity + iota((capacity, req_count), 0), 1.0, 0.0
        ).astype(BF16)
        place_ref[p] = place
        found = nt(digits, place)
        want_out[p] = (found[0:1] * 128.0 + found[1:2]).astype(jnp.int32)

    pl.semaphore_wait(barrier, peers - 1)

    def ask(step, carry):
        exchange(want_out, want_in, want_send, want_recv, step).start()
        return carry

    loop(ask)
    want_in[me] = want_out[me]

    highs = input_ref.shape[1] // 128
    for h in range(highs):
        lanes = slice(h * 128, (h + 1) * 128)
        upper, lower = halves(input_ref[:, lanes])
        table_ref[h * 16 : h * 16 + 8, 0:128] = upper
        table_ref[h * 16 : h * 16 + 8, 128:256] = lower
        coords = jnp.concatenate([pos_ref[:, lanes], jnp.zeros((5, 128), F32)], axis=0)
        upper, lower = halves(coords)
        table_ref[h * 16 + 8 : h * 16 + 16, 0:128] = upper
        table_ref[h * 16 + 8 : h * 16 + 16, 128:256] = lower

    def provide(peer):
        wanted = want_in[peer]
        one = jnp.where((wanted & 127) == iota((128, capacity), 0), 1.0, 0.0).astype(BF16)
        rows = nn(table_ref[...], jnp.concatenate([one, one], axis=0))
        rows = rows.reshape(highs, 16, capacity)
        chosen = (wanted >> 7) == iota((highs, 1, capacity), 0)
        rows = jnp.sum(jnp.where(chosen, rows, 0.0), axis=0)
        reply_out[peer] = rows[0 : reply_out.shape[1]]

    provide(me)

    def answer(step, carry):
        peer, got = arrival(want_in, want_send, want_recv, peers - step)
        got.wait_recv()
        provide(peer)
        exchange(reply_out, reply_in, reply_send, reply_recv, peers - step).start()
        return carry

    loop(answer)
    reply_in[me] = reply_out[me]

    counts = []
    ones = jnp.ones((16, BLOCK_PTS), BF16)
    per_pair = [nt(ones, mask_ref[j].astype(F32).astype(BF16))[0:1] for j in range(pairs)]
    for b in range(blocks):
        count = jnp.zeros((1, BLOCK_CELLS), F32)
        for j in range(pairs):
            count = count + jnp.where(pair_ref[j] == b, per_pair[j], 0.0)
        counts.append(count)
    divisor = jnp.maximum(jnp.concatenate(counts, axis=1), 1.0)
    gcells = cot_ref[...] / divisor
    index = iota((16, cells), 1)
    column = (lax.rem(index, GRID_ROW).astype(F32) + 0.5) / GRID_ROW
    row = (lax.div(index, GRID_ROW).astype(F32) + 0.5) * GRID_ROW / cells
    third = (me.astype(F32) + 0.5) / peers
    line = iota((16, cells), 0)
    coords = jnp.where(line == 0, column, jnp.where(line == 1, row, third))
    shifted = jnp.where(
        line == 3,
        column,
        jnp.where(
            line == 4, row, jnp.where(line == 5, third, jnp.where(line == 6, 1.0, 0.0))
        ),
    )
    first = first_ref[...]
    cell_weights = jnp.concatenate([first[3:7], jnp.zeros((4, width), F32)], axis=0)
    cell_values = jnp.where(line == 3, 1.0, jnp.where(line < 3, coords, 0.0))[0:8]
    cellpart = tn_exact(cell_weights, cell_values)
    for k in range(blocks * groups):
        turn = (cells - k * GROUP) % cells
        for value, into in ((cellpart, cellpart_ref), (gcells, gcell_ref), (shifted, cellrow_ref)):
            into[k] = pltpu.roll(value, turn, 1) if turn else value
    half_turned = second_ref[...].astype(F32) * 0.5
    half_second = half_turned.T.astype(BF16)
    half_turned = half_turned.astype(BF16)
    eight = jnp.concatenate([first, jnp.zeros((1, width), F32)], axis=0)
    coarse = eight.astype(BF16).astype(F32)
    wpre_ref[...] = jnp.concatenate(
        [
            coarse,
            jnp.where(iota((8, width), 0) < 3, coarse, 0.0),
            eight - coarse,
            jnp.zeros((8, width), F32),
        ],
        axis=0,
    ).T.astype(BF16)
    lat_ref[...] = jnp.zeros_like(lat_ref)
    dsec_ref[...] = jnp.zeros_like(dsec_ref)
    dfir_ref[...] = jnp.zeros_like(dfir_ref)
    dfeat_ref[...] = jnp.zeros_like(dfeat_ref)

    drain(reply_in, reply_recv)
    read = jnp.zeros((reply_in.shape[1], req_count), F32)
    for p in range(peers):
        upper, lower = halves(reply_in[p])
        read = read + (nn(upper, place_ref[p]) + nn(lower, place_ref[p]))
    inputs = read[0:8]
    points = jnp.concatenate([read[8:11], jnp.zeros((5, req_count), F32)], axis=0)
    req_z = tn_exact(lift_ref[...], inputs)
    gate = jax.nn.sigmoid(req_z)
    feats = req_z * gate
    slope = gate * (1.0 + req_z * (1.0 - gate))
    point_weights = jnp.concatenate([first[0:3], jnp.zeros((5, width), F32)], axis=0)
    pointpart = tn_exact(point_weights, points)
    upper = points.astype(BF16).astype(F32)
    both = jnp.concatenate([upper, points - upper], axis=0)
    for j in range(pairs):
        lanes = slice(j * BLOCK_PTS, (j + 1) * BLOCK_PTS)
        feat_ref[j] = feats[:, lanes]
        pointpart_ref[j] = pointpart[:, lanes]
        yrow_ref[j] = both[:, lanes]

    def work(step, carry):
        j = step // groups
        i = step % groups
        cell_block = pair_ref[j]
        at = cell_block * groups + i
        mask = mask_ref[j, pl.ds(pl.multiple_of(i * GROUP, GROUP), GROUP), :].astype(F32)
        feat = feat_ref[j]
        grads = gcell_ref[at]
        lane = iota((channels, cells), 1)
        rows_now = cellrow_ref[at]
        yrow = yrow_ref[j]

        def forward(s):
            both_lanes = slice(s * BLOCK_PTS, (s + 2) * BLOCK_PTS)
            for c in (s, s + 1):
                lanes = slice(c * BLOCK_PTS, (c + 1) * BLOCK_PTS)
                dk_ref[:, lanes] = ((feat * mask[c : c + 1]) * grads[:, c : c + 1]).astype(BF16)
                side = (yrow + rows_now[:, c : c + 1]).astype(BF16)
                side_ref[0:16, lanes] = side
                side_ref[16:32, lanes] = side
            dh_ref[:, both_lanes] = nn(half_second, dk_ref[:, both_lanes])
            pre = nn(wpre_ref[...], side_ref[:, both_lanes])
            for h in range(0, width, CHUNK):
                rows = slice(h, h + CHUNK)
                x = pre[rows].astype(BF16)
                square = x * x
                t = jnp.tanh(x * (A16 + B16 * square))
                u = ONE + t
                hid = x * u
                hid_ref[rows, both_lanes] = hid
                bend = hid * (ONE - t) * (A16 + C16 * square)
                dpre_ref[rows, both_lanes] = (u + bend) * dh_ref[rows, both_lanes].astype(BF16)

        def backward(s, lat, dfeat):
            both_lanes = slice(s * BLOCK_PTS, (s + 2) * BLOCK_PTS)
            kernels = nn(half_turned, hid_ref[:, both_lanes])
            for d in range(2):
                c = s + d
                masked = kernels[:, d * BLOCK_PTS : (d + 1) * BLOCK_PTS] * mask[c : c + 1]
                total = jnp.sum(masked * feat, axis=1, keepdims=True)
                lat = lat + jnp.where(
                    lane == cell_block * BLOCK_CELLS + i * GROUP + c, total, 0.0
                )
                dfeat = dfeat + masked * grads[:, c : c + 1]
            return lat, dfeat

        lat = jnp.zeros((channels, cells), F32)
        dfeat = jnp.zeros((channels, BLOCK_PTS), F32)
        for s in range(0, GROUP, 2):
            forward(s)
            if s:
                lat, dfeat = backward(s - 2, lat, dfeat)
        lat, dfeat = backward(GROUP - 2, lat, dfeat)
        lat_ref[...] += lat
        dfeat_ref[j] += dfeat
        dsec_ref[...] += nt(hid_ref[...], dk_ref[...])
        dfir_ref[...] += nt(side_ref[0:16], dpre_ref[...])
        return carry

    lax.fori_loop(0, pairs * groups, work, 0)

    latent_ref[...] = (lat_ref[...] / divisor).astype(BF16)
    dfeat = jnp.concatenate([dfeat_ref[j] for j in range(pairs)], axis=1)
    lift = nt(inputs, dfeat * slope, PREC)
    half = width // 2
    flat_ref[...] = jnp.zeros_like(flat_ref)
    dsec = dsec_ref[...].T * 0.5
    dfir = dfir_ref[0:8] + dfir_ref[8:16]
    flat_ref[0:channels] = dsec[:, :half]
    flat_ref[channels : 2 * channels] = dsec[:, half:]
    flat_ref[2 * channels : 2 * channels + 8] = dfir[:, :half]
    flat_ref[2 * channels + 8 : 2 * channels + 16] = dfir[:, half:]
    flat_ref[2 * channels + 16 : 2 * channels + 24, 0:channels] = lift
    for p in range(peers):
        part_out[p] = flat_ref[p * share : (p + 1) * share]

    def scatter(step, carry):
        exchange(part_out, part_in, part_send, part_recv, step).start()
        return carry

    loop(scatter)
    part_in[me] = part_out[me]

    drain(part_in, part_recv)
    total_out[...] = jnp.sum(part_in[...], axis=0)

    def spread(step):
        peer = lax.rem(me + step, peers)
        return pltpu.make_async_remote_copy(
            src_ref=total_out,
            dst_ref=total_in.at[me],
            send_sem=total_send,
            recv_sem=total_recv,
            device_id={"slab": peer},
        )

    def give(step, carry):
        spread(step).start()
        return carry

    loop(give)
    total_in[me] = total_out[...]

    drain(total_in, total_recv)
    drain(want_in, want_send)
    drain(reply_in, reply_send)
    drain(part_in, part_send)
    drain(total_in, total_send)
    for p in range(peers):
        flat_ref[p * share : (p + 1) * share] = total_in[p]
    gsecond_ref[:, 0:half] = flat_ref[0:channels]
    gsecond_ref[:, half:width] = flat_ref[channels : 2 * channels]
    gfirst_ref[:, 0:half] = flat_ref[2 * channels : 2 * channels + 7]
    gfirst_ref[:, half:width] = flat_ref[2 * channels + 8 : 2 * channels + 15]
    glift_ref[...] = flat_ref[2 * channels + 16 : 2 * channels + 24, 0:channels]


def per_device(
    point_pos,
    point_input,
    req_owner,
    req_local,
    pair_cell,
    pair_mask,
    w_first,
    w_second,
    w_lift,
    cotangent,
):
    peers = lax.axis_size("slab")
    req_count = req_local.shape[0]
    capacity = 4 * req_count // peers
    channels, cells = cotangent.shape
    width = w_first.shape[1]
    pairs = pair_mask.shape[0]
    points = point_input.shape[1]
    rows = point_input.shape[0] + point_pos.shape[0]
    kinds = cells // GROUP
    share = -(-(2 * channels + 24) // peers)
    span = GROUP * BLOCK_PTS
    vmem = pl.BlockSpec(memory_space=pltpu.VMEM)
    one = pltpu.SemaphoreType.DMA
    sems = [one, pltpu.SemaphoreType.DMA((peers,))] + [one] * 6
    latent, gfirst, gsecond, glift = pl.pallas_call(
        functools.partial(body, peers),
        out_shape=(
            jax.ShapeDtypeStruct((channels, cells), BF16),
            jax.ShapeDtypeStruct(w_first.shape, F32),
            jax.ShapeDtypeStruct(w_second.shape[::-1], F32),
            jax.ShapeDtypeStruct(w_lift.shape, F32),
        ),
        in_specs=[vmem] * 4 + [pl.BlockSpec(memory_space=pltpu.SMEM)] + [vmem] * 5,
        out_specs=[vmem] * 4,
        scratch_shapes=[
            pltpu.VMEM((peers, capacity, req_count), BF16),
            pltpu.VMEM((peers, 1, capacity), jnp.int32),
            pltpu.VMEM((peers, 1, capacity), jnp.int32),
            pltpu.VMEM((points // 128 * 16, 256), BF16),
            pltpu.VMEM((peers, rows, capacity), F32),
            pltpu.VMEM((peers, rows, capacity), F32),
            pltpu.VMEM((kinds, width, cells), F32),
            pltpu.VMEM((kinds, channels, cells), F32),
            pltpu.VMEM((kinds, 16, cells), F32),
            pltpu.VMEM((pairs, width, BLOCK_PTS), F32),
            pltpu.VMEM((pairs, channels, BLOCK_PTS), F32),
            pltpu.VMEM((pairs, 16, BLOCK_PTS), F32),
            pltpu.VMEM((channels, span), BF16),
            pltpu.VMEM((width, span), F32),
            pltpu.VMEM((width, span), BF16),
            pltpu.VMEM((width, span), BF16),
            pltpu.VMEM((32, span), BF16),
            pltpu.VMEM((width, 32), BF16),
            pltpu.VMEM((channels, cells), F32),
            pltpu.VMEM((pairs, channels, BLOCK_PTS), F32),
            pltpu.VMEM((width, channels), F32),
            pltpu.VMEM((16, width), F32),
            pltpu.VMEM((peers * share, 128), F32),
            pltpu.VMEM((peers, share, 128), F32),
            pltpu.VMEM((peers, share, 128), F32),
            pltpu.VMEM((share, 128), F32),
            pltpu.VMEM((peers, share, 128), F32),
        ]
        + sems,
        compiler_params=pltpu.CompilerParams(
            collective_id=0, has_side_effects=True, vmem_limit_bytes=60 * 1024 * 1024
        ),
    )(
        point_pos,
        point_input,
        req_owner.reshape(1, req_count),
        req_local.reshape(1, req_count),
        pair_cell,
        pair_mask,
        w_first,
        w_second.T,
        w_lift,
        cotangent,
    )
    return latent, gfirst, gsecond.T, glift


def solution(mesh):
    split = ("groups", "slab")
    in_specs = (
        P(None, split),
        P(None, split),
        P(split, None),
        P(split),
        P(split),
        P(split, None, None),
        P(),
        P(),
        P(),
        P(None, split),
    )
    out_specs = (P(None, split), P("groups", None), P("groups", None), P("groups", None))
    return jax.shard_map(
        per_device, mesh=mesh, in_specs=in_specs, out_specs=out_specs, check_vma=False
    )
```

```python
import functools

import ml_dtypes
import numpy as np
import jax
import jax.numpy as jnp
from jax import lax
from jax.experimental import pallas as pl
from jax.experimental.pallas import tpu as pltpu
from jax.sharding import PartitionSpec as P

BLOCK_PTS = 128
BLOCK_CELLS = 64
GRID_ROW = 16
GROUP = 8
CHUNK = 64
GELU_A = 0.7978845608028654
GELU_B = 0.044715 / GELU_A**2

ONE = np.array(1.0, ml_dtypes.bfloat16)
B16 = np.array(GELU_B, ml_dtypes.bfloat16)
C16 = np.array(3.0*GELU_B, ml_dtypes.bfloat16)
PREC = lax.Precision.HIGHEST
F32 = jnp.float32
BF16 = jnp.bfloat16


def nn(a, b):
    return lax.dot_general(a, b, (((1,), (0,)), ((), ())), preferred_element_type=F32)


def nt(a, b, precision=None):
    return lax.dot_general(
        a, b, (((1,), (1,)), ((), ())), precision=precision, preferred_element_type=F32
    )


def tn_exact(a, b):
    return lax.dot_general(
        a, b, (((0,), (0,)), ((), ())), precision=PREC, preferred_element_type=F32
    )


def halves(value):
    high = value.astype(BF16)
    return high, (value - high.astype(F32)).astype(BF16)


def iota(shape, axis):
    return lax.broadcasted_iota(jnp.int32, shape, axis)


def body(
    peers,
    pos_ref,
    input_ref,
    owner_ref,
    local_ref,
    pair_ref,
    mask_ref,
    first_ref,
    second_ref,
    lift_ref,
    cot_ref,
    latent_ref,
    gfirst_ref,
    gsecond_ref,
    glift_ref,
    place_ref,
    want_out,
    want_in,
    table_ref,
    reply_out,
    reply_in,
    gcell_ref,
    cellrow_ref,
    feat_ref,
    yrow_ref,
    dk_ref,
    dh_ref,
    hid_ref,
    dpre_ref,
    side_ref,
    wpre_ref,
    lat_ref,
    dfeat_ref,
    dsec_ref,
    dfir_ref,
    flat_ref,
    part_out,
    part_in,
    total_out,
    total_in,
    want_send,
    want_recv,
    reply_send,
    reply_recv,
    part_send,
    part_recv,
    total_send,
    total_recv,
):
    me = lax.axis_index("slab")
    req_count = local_ref.shape[1]
    capacity = want_in.shape[2]
    pairs = mask_ref.shape[0]
    cells = cot_ref.shape[1]
    blocks = cells // BLOCK_CELLS
    groups = BLOCK_CELLS // GROUP
    channels = cot_ref.shape[0]
    width = first_ref.shape[1]
    share = part_in.shape[1]

    barrier = pltpu.get_barrier_semaphore()

    def loop(act):
        lax.fori_loop(1, peers, act, 0, unroll=1)

    def greet(step, carry):
        peer = lax.rem(me + step, peers)
        pl.semaphore_signal(barrier, inc=1, device_id={"slab": peer})
        return carry

    loop(greet)

    def exchange(source, target, send, recv, step):
        peer = lax.rem(me + step, peers)
        return pltpu.make_async_remote_copy(
            src_ref=source.at[peer],
            dst_ref=target.at[me],
            send_sem=send,
            recv_sem=recv.at[me] if recv is want_recv else recv,
            device_id={"slab": peer},
        )

    def drain(like, sem):
        part = like.at[pl.ds(0, peers - 1)]
        pltpu.make_async_copy(part, part, sem).wait()

    def arrival(target, send, recv, step):
        peer = lax.rem(me + step, peers)
        return peer, pltpu.make_async_remote_copy(
            src_ref=target.at[peer],
            dst_ref=target.at[peer],
            send_sem=send,
            recv_sem=recv.at[peer],
            device_id={"slab": peer},
        )

    owner = owner_ref[...]
    local = local_ref[...]
    named = jnp.where(owner == iota((peers, req_count), 0), 1.0, 0.0)
    earlier = jnp.where(
        iota((req_count, req_count), 0) < iota((req_count, req_count), 1), 1.0, 0.0
    ).astype(BF16)
    rank = jnp.sum(named * nn(named.astype(BF16), earlier), axis=0, keepdims=True)
    slot = owner * capacity + rank.astype(jnp.int32)
    line = iota((16, req_count), 0)
    digits = jnp.where(
        line == 0, local >> 7, jnp.where(line == 1, local & 127, 0)
    ).astype(F32).astype(BF16)
    for p in range(peers):
        place = jnp.where(
            slot == p * capacity + iota((capacity, req_count), 0), 1.0, 0.0
        ).astype(BF16)
        place_ref[p] = place
        found = nt(digits, place)
        want_out[p] = (found[0:1] * 128.0 + found[1:2]).astype(jnp.int32)

    pl.semaphore_wait(barrier, peers - 1)

    def ask(step, carry):
        exchange(want_out, want_in, want_send, want_recv, step).start()
        return carry

    loop(ask)
    want_in[me] = want_out[me]

    highs = input_ref.shape[1] // 128
    for h in range(highs):
        lanes = slice(h * 128, (h + 1) * 128)
        upper, lower = halves(input_ref[:, lanes])
        table_ref[h * 16 : h * 16 + 8, 0:128] = upper
        table_ref[h * 16 : h * 16 + 8, 128:256] = lower
        coords = jnp.concatenate([pos_ref[:, lanes], jnp.zeros((5, 128), F32)], axis=0)
        upper, lower = halves(coords)
        table_ref[h * 16 + 8 : h * 16 + 16, 0:128] = upper
        table_ref[h * 16 + 8 : h * 16 + 16, 128:256] = lower

    def provide(peer):
        wanted = want_in[peer]
        one = jnp.where((wanted & 127) == iota((128, capacity), 0), 1.0, 0.0).astype(BF16)
        rows = nn(table_ref[...], jnp.concatenate([one, one], axis=0))
        rows = rows.reshape(highs, 16, capacity)
        chosen = (wanted >> 7) == iota((highs, 1, capacity), 0)
        rows = jnp.sum(jnp.where(chosen, rows, 0.0), axis=0)
        reply_out[peer] = rows[0 : reply_out.shape[1]]

    provide(me)

    def answer(step, carry):
        peer, got = arrival(want_in, want_send, want_recv, peers - step)
        got.wait_recv()
        provide(peer)
        exchange(reply_out, reply_in, reply_send, reply_recv, peers - step).start()
        return carry

    loop(answer)
    reply_in[me] = reply_out[me]

    counts = []
    ones = jnp.ones((16, BLOCK_PTS), BF16)
    per_pair = [nt(ones, mask_ref[j].astype(F32).astype(BF16))[0:1] for j in range(pairs)]
    for b in range(blocks):
        count = jnp.zeros((1, BLOCK_CELLS), F32)
        for j in range(pairs):
            count = count + jnp.where(pair_ref[j] == b, per_pair[j], 0.0)
        counts.append(count)
    divisor = jnp.maximum(jnp.concatenate(counts, axis=1), 1.0)
    gcells = cot_ref[...] / divisor
    index = iota((16, cells), 1)
    column = (lax.rem(index, GRID_ROW).astype(F32) + 0.5) / GRID_ROW
    row = (lax.div(index, GRID_ROW).astype(F32) + 0.5) * GRID_ROW / cells
    third = (me.astype(F32) + 0.5) / peers
    line = iota((16, cells), 0)
    shifted = jnp.where(
        line == 3,
        column,
        jnp.where(
            line == 4, row, jnp.where(line == 5, third, jnp.where(line == 6, 1.0, 0.0))
        ),
    )
    first = first_ref[...]
    for k in range(blocks * groups):
        turn = (cells - k * GROUP) % cells
        for value, into in ((gcells, gcell_ref), (shifted, cellrow_ref)):
            into[k] = pltpu.roll(value, turn, 1) if turn else value
    half_turned = second_ref[...].astype(F32) * 0.5
    half_second = half_turned.T.astype(BF16)
    half_turned = half_turned.astype(BF16)
    eight = jnp.concatenate([first, jnp.zeros((1, width), F32)], axis=0) * GELU_A
    coarse = eight.astype(BF16).astype(F32)
    wpre_ref[...] = jnp.concatenate(
        [
            coarse,
            jnp.where(iota((8, width), 0) < 3, coarse, 0.0),
            eight - coarse,
            jnp.zeros((8, width), F32),
        ],
        axis=0,
    ).T.astype(BF16)
    lat_ref[...] = jnp.zeros_like(lat_ref)
    dsec_ref[...] = jnp.zeros_like(dsec_ref)
    dfir_ref[...] = jnp.zeros_like(dfir_ref)
    dfeat_ref[...] = jnp.zeros_like(dfeat_ref)

    drain(reply_in, reply_recv)
    read = jnp.zeros((reply_in.shape[1], req_count), F32)
    for p in range(peers):
        upper, lower = halves(reply_in[p])
        read = read + (nn(upper, place_ref[p]) + nn(lower, place_ref[p]))
    inputs = read[0:8]
    points = jnp.concatenate([read[8:11], jnp.zeros((5, req_count), F32)], axis=0)
    req_z = tn_exact(lift_ref[...], inputs)
    gate = jax.nn.sigmoid(req_z)
    feats = req_z * gate
    slope = gate * (1.0 + req_z * (1.0 - gate))
    upper = points.astype(BF16).astype(F32)
    both = jnp.concatenate([upper, points - upper], axis=0)
    for j in range(pairs):
        lanes = slice(j * BLOCK_PTS, (j + 1) * BLOCK_PTS)
        feat_ref[j] = feats[:, lanes]
        yrow_ref[j] = both[:, lanes]

    def work(step, carry):
        j = step // groups
        i = step % groups
        cell_block = pair_ref[j]
        at = cell_block * groups + i
        mask = mask_ref[j, pl.ds(pl.multiple_of(i * GROUP, GROUP), GROUP), :].astype(F32)
        feat = feat_ref[j]
        grads = gcell_ref[at]
        lane = iota((channels, cells), 1)
        rows_now = cellrow_ref[at]
        yrow = yrow_ref[j]

        def forward(s):
            both_lanes = slice(s * BLOCK_PTS, (s + 2) * BLOCK_PTS)
            for c in (s, s + 1):
                lanes = slice(c * BLOCK_PTS, (c + 1) * BLOCK_PTS)
                dk_ref[:, lanes] = ((feat * mask[c : c + 1]) * grads[:, c : c + 1]).astype(BF16)
                side = (yrow + rows_now[:, c : c + 1]).astype(BF16)
                side_ref[0:16, lanes] = side
                side_ref[16:32, lanes] = side
            dh_ref[:, both_lanes] = nn(half_second, dk_ref[:, both_lanes])
            pre = nn(wpre_ref[...], side_ref[:, both_lanes])
            for h in range(0, width, CHUNK):
                rows = slice(h, h + CHUNK)
                x = pre[rows].astype(BF16)
                square = x * x
                t = jnp.tanh(x * (ONE + B16 * square))
                u = ONE + t
                hid = x * u
                hid_ref[rows, both_lanes] = hid
                bend = hid * (ONE - t) * (ONE + C16 * square)
                dpre_ref[rows, both_lanes] = (u + bend) * dh_ref[rows, both_lanes].astype(BF16)

        def backward(s, lat, dfeat):
            both_lanes = slice(s * BLOCK_PTS, (s + 2) * BLOCK_PTS)
            kernels = nn(half_turned, hid_ref[:, both_lanes])
            for d in range(2):
                c = s + d
                masked = kernels[:, d * BLOCK_PTS : (d + 1) * BLOCK_PTS] * mask[c : c + 1]
                total = jnp.sum(masked * feat, axis=1, keepdims=True)
                lat = lat + jnp.where(
                    lane == cell_block * BLOCK_CELLS + i * GROUP + c, total, 0.0
                )
                dfeat = dfeat + masked * grads[:, c : c + 1]
            return lat, dfeat

        lat = jnp.zeros((channels, cells), F32)
        dfeat = jnp.zeros((channels, BLOCK_PTS), F32)
        for s in range(0, GROUP, 2):
            forward(s)
            if s:
                lat, dfeat = backward(s - 2, lat, dfeat)
        lat, dfeat = backward(GROUP - 2, lat, dfeat)
        lat_ref[...] += lat
        dfeat_ref[j] += dfeat
        dsec_ref[...] += nt(hid_ref[...], dk_ref[...])
        dfir_ref[...] += nt(side_ref[0:16], dpre_ref[...])
        return carry

    lax.fori_loop(0, pairs * groups, work, 0, unroll=4)

    latent_ref[...] = (lat_ref[...] / (divisor * GELU_A)).astype(BF16)
    dfeat = jnp.concatenate([dfeat_ref[j] for j in range(pairs)], axis=1) * (1.0 / GELU_A)
    lift = nt(inputs, dfeat * slope, PREC)
    half = width // 2
    flat_ref[...] = jnp.zeros_like(flat_ref)
    dsec = dsec_ref[...].T * (0.5 / GELU_A)
    dfir = dfir_ref[0:8] + dfir_ref[8:16]
    flat_ref[0:channels] = dsec[:, :half]
    flat_ref[channels : 2 * channels] = dsec[:, half:]
    flat_ref[2 * channels : 2 * channels + 8] = dfir[:, :half]
    flat_ref[2 * channels + 8 : 2 * channels + 16] = dfir[:, half:]
    flat_ref[2 * channels + 16 : 2 * channels + 24, 0:channels] = lift
    for p in range(peers):
        part_out[p] = flat_ref[p * share : (p + 1) * share]

    def scatter(step, carry):
        exchange(part_out, part_in, part_send, part_recv, step).start()
        return carry

    loop(scatter)
    part_in[me] = part_out[me]

    drain(part_in, part_recv)
    total_out[...] = jnp.sum(part_in[...], axis=0)

    def spread(step):
        peer = lax.rem(me + step, peers)
        return pltpu.make_async_remote_copy(
            src_ref=total_out,
            dst_ref=total_in.at[me],
            send_sem=total_send,
            recv_sem=total_recv,
            device_id={"slab": peer},
        )

    def give(step, carry):
        spread(step).start()
        return carry

    loop(give)
    total_in[me] = total_out[...]

    drain(total_in, total_recv)
    drain(want_in, want_send)
    drain(reply_in, reply_send)
    drain(part_in, part_send)
    drain(total_in, total_send)
    for p in range(peers):
        flat_ref[p * share : (p + 1) * share] = total_in[p]
    gsecond_ref[:, 0:half] = flat_ref[0:channels]
    gsecond_ref[:, half:width] = flat_ref[channels : 2 * channels]
    gfirst_ref[:, 0:half] = flat_ref[2 * channels : 2 * channels + 7]
    gfirst_ref[:, half:width] = flat_ref[2 * channels + 8 : 2 * channels + 15]
    glift_ref[...] = flat_ref[2 * channels + 16 : 2 * channels + 24, 0:channels]


def hand_out(*refs):
    for source, target in zip(refs[:4], refs[4:]):
        target[...] = source[...]


def per_device(
    point_pos,
    point_input,
    req_owner,
    req_local,
    pair_cell,
    pair_mask,
    w_first,
    w_second,
    w_lift,
    cotangent,
):
    peers = lax.axis_size("slab")
    req_count = req_local.shape[0]
    capacity = 4 * req_count // peers
    channels, cells = cotangent.shape
    width = w_first.shape[1]
    pairs = pair_mask.shape[0]
    points = point_input.shape[1]
    rows = point_input.shape[0] + point_pos.shape[0]
    kinds = cells // GROUP
    share = -(-(2 * channels + 24) // peers)
    span = GROUP * BLOCK_PTS
    vmem = pl.BlockSpec(memory_space=pltpu.VMEM)
    one = pltpu.SemaphoreType.DMA
    sems = [one, pltpu.SemaphoreType.DMA((peers,))] + [one] * 6
    latent, gfirst, gsecond, glift = pl.pallas_call(
        functools.partial(body, peers),
        out_shape=(
            jax.ShapeDtypeStruct((channels, cells), BF16),
            jax.ShapeDtypeStruct(w_first.shape, F32),
            jax.ShapeDtypeStruct(w_second.shape[::-1], F32),
            jax.ShapeDtypeStruct(w_lift.shape, F32),
        ),
        in_specs=[vmem] * 4 + [pl.BlockSpec(memory_space=pltpu.SMEM)] + [vmem] * 5,
        out_specs=[vmem] * 4,
        scratch_shapes=[
            pltpu.VMEM((peers, capacity, req_count), BF16),
            pltpu.VMEM((peers, 1, capacity), jnp.int32),
            pltpu.VMEM((peers, 1, capacity), jnp.int32),
            pltpu.VMEM((points // 128 * 16, 256), BF16),
            pltpu.VMEM((peers, rows, capacity), F32),
            pltpu.VMEM((peers, rows, capacity), F32),
            pltpu.VMEM((kinds, channels, cells), F32),
            pltpu.VMEM((kinds, 16, cells), F32),
            pltpu.VMEM((pairs, channels, BLOCK_PTS), F32),
            pltpu.VMEM((pairs, 16, BLOCK_PTS), F32),
            pltpu.VMEM((channels, span), BF16),
            pltpu.VMEM((width, span), F32),
            pltpu.VMEM((width, span), BF16),
            pltpu.VMEM((width, span), BF16),
            pltpu.VMEM((32, span), BF16),
            pltpu.VMEM((width, 32), BF16),
            pltpu.VMEM((channels, cells), F32),
            pltpu.VMEM((pairs, channels, BLOCK_PTS), F32),
            pltpu.VMEM((width, channels), F32),
            pltpu.VMEM((16, width), F32),
            pltpu.VMEM((peers * share, 128), F32),
            pltpu.VMEM((peers, share, 128), F32),
            pltpu.VMEM((peers, share, 128), F32),
            pltpu.VMEM((share, 128), F32),
            pltpu.VMEM((peers, share, 128), F32),
        ]
        + sems,
        compiler_params=pltpu.CompilerParams(
            collective_id=0, has_side_effects=True, vmem_limit_bytes=60 * 1024 * 1024
        ),
    )(
        point_pos,
        point_input,
        req_owner.reshape(1, req_count),
        req_local.reshape(1, req_count),
        pair_cell,
        pair_mask,
        w_first,
        w_second.T,
        w_lift,
        cotangent,
    )
    results = (latent, gfirst, gsecond, glift)
    latent, gfirst, gsecond, glift = pl.pallas_call(
        hand_out,
        out_shape=tuple(jax.ShapeDtypeStruct(r.shape, r.dtype) for r in results),
        in_specs=[vmem] * 4,
        out_specs=[vmem] * 4,
    )(*results)
    return latent, gfirst, gsecond.T, glift


def solution(mesh):
    split = ("groups", "slab")
    in_specs = (
        P(None, split),
        P(None, split),
        P(split, None),
        P(split),
        P(split),
        P(split, None, None),
        P(),
        P(),
        P(),
        P(None, split),
    )
    out_specs = (P(None, split), P("groups", None), P("groups", None), P("groups", None))
    return jax.shard_map(
        per_device, mesh=mesh, in_specs=in_specs, out_specs=out_specs, check_vma=False
    )
```
